512 devices in a mesh: tm: 32 (over x, z_lo), seq: 16 (over y, z_hi, core).
Axes of the slice: x: 4, y: 4, z: 16 (z_hi: 2, z_lo: 8; z = z_hi * 8 + z_lo), core: 2. Of those that a mesh axis runs over, the one named last changes fastest.
Arguments:
- x_start: float32 [2048, 64], P('seq')
- old_states: float32 [32, 2048, 64], P('tm', 'seq')
- hidden: bfloat16 [32, 2048, 2560], P('tm', 'seq')
- modulation: float32 [51, 2, 2560], replicated, may hold values from -4 to 4
- step_index: int32 [32], replicated, may hold values from 0 to 49, as said below
- sigma_table: float32 [51], replicated, may hold values from 0 to 1, as said below
- w_query: bfloat16 [2560, 2048], P(None, 'seq')
- w_key: bfloat16 [2560, 2048], P(None, 'seq')
- w_value: bfloat16 [2560, 2048], P(None, 'seq'), may hold values from -0.125 to 0.125
- qk_gain: float32 [2, 2048], P(None, 'seq'), may hold values from 0.8 to 7.2
- w_head: bfloat16 [2048, 64], replicated, may hold values from -0.5 to 0.5
- w_skip: bfloat16 [2560, 64], replicated, may hold values from -0.125 to 0.125
Outputs:
- drift: float32 [32, 2048, 64], P('tm', 'seq')
- new_states: float32 [32, 2048, 64], P('tm', 'seq')
- error: float32 [32], P('tm')
The draws below stay inside these ranges and needn't reach their ends.
Inputs may be any that keep to these rules, and one draw needn't show every extreme that they name: `step_index`: strictly increasing; the first is 0 and the last 49. `sigma_table`: falls from step to step.
All inputs are finite; a program needn't handle non-finite values.
Results may differ from the reference program's by a relative error of at most 0.009.
Values may be sent and summed in bfloat16 or wider, within the bound.
No kernel may reach another device: no remote copies, remote signals or barrier semaphores. Data moves between devices by JAX's collectives and lax.ppermute only.
A program may use at most 64 MiB of HBM per device.

```python
import jax
import jax.numpy as jnp
from jax import lax

D = 2560
HD = 64
LAT = 64
STEPS = 50
TOK_DEV = 128
WINDOW = 32
TOKENS = 2048
HEADS = 32


def column_ramp(columns, lower, upper):
    position = jnp.arange(columns, dtype=jnp.float32)
    return lower + (upper - lower) * position / max(columns - 1, 1)


def shared_columns(key):
    return jax.random.truncated_normal(key, -4.0, 4.0, (D, HEADS * HD), jnp.float32)


def start_field(key):
    first = jax.random.fold_in(key, 0)
    normal_part = jax.random.truncated_normal(first, -5.0, 5.0, (TOKENS, LAT), jnp.float32)
    return normal_part


def region_weights(key, regions):
    order = jax.random.permutation(key, regions)
    return jnp.where(order < regions // 3, 1.0, 0.25).astype(jnp.float32)


def draw_x_start(key, part):
    base = start_field(key)
    return base


def draw_old_states(key, part):
    base = start_field(key)
    key = jax.random.fold_in(key, 12)
    first = jax.random.fold_in(key, 0)
    shape = (WINDOW, TOKENS, LAT)
    wobble = 0.25 * jax.random.truncated_normal(first, -5.0, 5.0, shape, jnp.float32)
    return base[None] + wobble


def draw_w_query(key, part):
    base = shared_columns(key)
    return (base * column_ramp(HEADS * HD, 0.6, 1.8) * D ** (-0.5)).astype(jnp.bfloat16)


def draw_w_key(key, part):
    key = jax.random.fold_in(key, 22)
    own = jax.random.truncated_normal(key, -4.0, 4.0, (D, HEADS * HD), jnp.float32)
    return (own * column_ramp(HEADS * HD, 0.6, 1.8) * D ** (-0.5)).astype(jnp.bfloat16)


def draw_qk_gain(key, part):
    key = jax.random.fold_in(key, 31)
    columns = HEADS * HD
    return jax.random.uniform(key, (2, columns), jnp.float32, 1.0, 2.0)


def draw_hidden(key, part):
    key = jax.random.fold_in(key, 11)
    first = jax.random.fold_in(key, 0)
    fifth = jax.random.fold_in(key, 4)
    sixth = jax.random.fold_in(key, 5)
    shape = (WINDOW, TOKENS, D)
    width = max(TOK_DEV // 2, 1)
    regions = TOKENS // width
    weight = jnp.repeat(region_weights(fifth, regions), width)[None, :, None]
    fresh_share = jnp.sqrt(1.0 - weight * weight)
    flat = jax.random.truncated_normal(first, -6.0, 6.0, shape, jnp.float32)
    still = jax.random.truncated_normal(sixth, -6.0, 6.0, (1, TOKENS, D), jnp.float32)
    return (weight * still + fresh_share * flat).astype(jnp.bfloat16)


def draw_step_index(key, part):
    key = jax.random.fold_in(key, 41)
    inner = jax.random.permutation(key, STEPS - 2)[:WINDOW - 2].astype(jnp.int32) + 1
    ends = jnp.array([0, STEPS - 1], dtype=jnp.int32)
    return jnp.sort(jnp.concatenate([ends, inner]))


def draw_sigma_table(key, part):
    key = jax.random.fold_in(key, 51)
    first, second = jax.random.split(key)
    position = jnp.arange(STEPS + 1, dtype=jnp.float32)
    jitter = jax.random.uniform(first, (STEPS + 1,), jnp.float32, 0.0, 0.8)
    drawn = jnp.clip((STEPS - position + jitter) / STEPS, 0.0, 1.0)
    shift_value = jax.random.uniform(second, (), jnp.float32, 2.0, 8.0)
    return shift_value * drawn / (1.0 + (shift_value - 1.0) * drawn)


def block_levels(rng, dims, cuts, low, largest):
    level = 1.0
    for dim, blocks in cuts:
        draws = jax.random.uniform(jax.random.fold_in(jax.random.fold_in(rng, 6), dim), (blocks,), jnp.float32, low / len(cuts), largest / len(cuts))
        level = level * jnp.repeat(jnp.exp(draws), dims[dim] // blocks).reshape((-1,) + (1,) * (len(dims) - 1 - dim))
    return level


def normal_values(stream_key, dims, deviation, most, shards=(), kind=jnp.bfloat16):
    level = block_levels(stream_key, dims, shards, -0.22, 0.18) if shards else 1.0
    values = jax.random.normal(stream_key, dims, jnp.float32) * deviation * level
    return jnp.minimum(jnp.maximum(values, -most), most).astype(kind)


def setup_inputs(seed: int = 0) -> dict:
    seeds = jax.random.split(jax.random.key(seed), 13)
    x_start = draw_x_start(jax.random.fold_in(seeds[12], 71), 0)
    old_states = draw_old_states(jax.random.fold_in(seeds[12], 71), 0)
    hidden = draw_hidden(jax.random.fold_in(seeds[12], 71), 0)
    modulation = normal_values(seeds[3], (STEPS + 1, 2, D), 0.3, 4.0, (), jnp.float32)
    step_index = draw_step_index(jax.random.fold_in(seeds[12], 71), 0)
    sigma_table = draw_sigma_table(jax.random.fold_in(seeds[12], 71), 0)
    w_query = draw_w_query(jax.random.fold_in(seeds[12], 71), 0)
    w_key = draw_w_key(jax.random.fold_in(seeds[12], 71), 0)
    w_value = normal_values(seeds[8], (D, HEADS * HD), D ** -0.5, 0.125, ((1, 16),))
    qk_gain = draw_qk_gain(jax.random.fold_in(seeds[12], 71), 0)
    w_head = normal_values(seeds[10], (HEADS * HD, LAT), ((HEADS * HD) // 16) ** -0.5, 0.5)
    w_skip = normal_values(seeds[11], (D, LAT), D ** -0.5, 0.125)
    return {"x_start": x_start, "old_states": old_states, "hidden": hidden, "modulation": modulation, "step_index": step_index, "sigma_table": sigma_table, "w_query": w_query, "w_key": w_key, "w_value": w_value, "qk_gain": qk_gain, "w_head": w_head, "w_skip": w_skip}


def layer_norm(token_rows):
    average = lax.optimization_barrier(jnp.mean(token_rows, axis=-1, keepdims=True))
    centred = token_rows - average
    spread = lax.optimization_barrier(jnp.mean(centred * centred, axis=-1, keepdims=True))
    return centred * lax.rsqrt(spread + 1e-06)

def unit_rows(values, gain_row):
    power = lax.optimization_barrier(jnp.mean(values * values, axis=-1, keepdims=True))
    return (values * lax.rsqrt(power + 1e-06) * gain_row).astype(jnp.bfloat16)

def head_attention(triple):
    query_head, key_head, value_head = triple
    scores = jnp.dot(query_head.astype(jnp.float32), key_head.astype(jnp.float32).T) * HD ** (-0.5)
    highest = lax.optimization_barrier(jnp.max(scores, axis=-1, keepdims=True))
    raised = jnp.exp(scores - highest)
    summed = lax.optimization_barrier(jnp.sum(raised, axis=-1, keepdims=True))
    output = jnp.dot(raised.astype(jnp.bfloat16), value_head, preferred_element_type=jnp.float32) / summed
    return output.astype(jnp.bfloat16)

def reference(x_start, old_states, hidden, modulation, step_index, sigma_table, w_query, w_key, w_value, qk_gain, w_head, w_skip):
    following = jnp.concatenate([step_index[1:], step_index[-1:] + 1]).astype(jnp.int32)
    delta = sigma_table[following] - sigma_table[step_index]
    mod_rows = modulation[step_index]

    def split_heads(values):
        return values.reshape(TOKENS, HEADS, HD).transpose(1, 0, 2)

    def drift_one(pair):
        token_rows, mod_now = pair
        normed = (layer_norm(token_rows.astype(jnp.float32)) * (1.0 + mod_now[0]) + mod_now[1]).astype(jnp.bfloat16)
        query = jnp.dot(normed, w_query, preferred_element_type=jnp.float32)
        key_proj = jnp.dot(normed, w_key, preferred_element_type=jnp.float32)
        value_proj = jnp.dot(normed, w_value, preferred_element_type=jnp.float32)
        query_unit = unit_rows(query, qk_gain[0])
        key_unit = unit_rows(key_proj, qk_gain[1])
        value_unit = value_proj.astype(jnp.bfloat16)
        per_head = lax.map(head_attention, (split_heads(query_unit), split_heads(key_unit), split_heads(value_unit)))
        attended = per_head.transpose(1, 0, 2).reshape(TOKENS, HEADS * HD)
        return jnp.dot(attended, w_head, preferred_element_type=jnp.float32) + jnp.dot(normed, w_skip, preferred_element_type=jnp.float32)
    drift = lax.map(drift_one, (hidden, mod_rows))
    increments = delta[:, None, None] * drift
    new_states = x_start[None] + jnp.cumsum(increments, axis=0)
    change = new_states - old_states
    error = lax.optimization_barrier(jnp.mean(change * change, axis=(1, 2)))
    return (drift, new_states, error)
```

```python
import functools
import math

import jax
import jax.numpy as jnp
from jax import lax
from jax.experimental import pallas as pl
from jax.experimental.pallas import tpu as pltpu
from jax.sharding import PartitionSpec as P

HD = 64
Y, Z, C = 4, 2, 2
ZL = 8
OFFSETS = (0, -1, 1, 2)
CHUNKS = ((0, 64), (64, 128))


def seq_perm(move):
    pairs = []
    for s in range(Y * Z * C):
        y, z, c = s // (Z * C), (s // C) % Z, s % C
        y, z, c = move(y, z, c)
        pairs.append((s, ((y % Y) * Z + z) * C + c))
    return pairs


TO_CORE = seq_perm(lambda y, z, c: (y, z, 1 - c))
TO_UP = seq_perm(lambda y, z, c: (y + 1, z, c))
TO_DOWN = seq_perm(lambda y, z, c: (y - 1, z, c))
TO_FAR = seq_perm(lambda y, z, c: (y, 1 - z, c))


def along_y(rows):
    half = rows.shape[0] // 2
    below = lax.ppermute(rows, "seq", TO_UP)
    above = lax.ppermute(rows, "seq", TO_DOWN)
    opposite = (
        lax.ppermute(below[:half], "seq", TO_UP),
        lax.ppermute(above[half:], "seq", TO_DOWN),
    )
    return (rows, below, above) + opposite


def project_kernel(
    place_ref, scale_ref, shift_ref, w_ref, own_ref, below_ref, above_ref, first_ref, second_ref,
    mine_ref, other_ref, power_ref, normed_ref,
):
    count = own_ref.shape[0]
    spots = (
        (own_ref, 0), (below_ref, count), (above_ref, 2 * count),
        (first_ref, 3 * count), (second_ref, 3 * count + count // 2),
    )
    scale = 1.0 + scale_ref[...]
    shift = shift_ref[...]
    for ref, start in spots:
        rows = ref[...].astype(jnp.float32)
        average = jnp.mean(rows, axis=-1, keepdims=True)
        centred = rows - average
        spread = jnp.mean(centred * centred, axis=-1, keepdims=True)
        normed = centred * lax.rsqrt(spread + 1e-6) * scale + shift
        normed_ref[start : start + ref.shape[0], :] = normed.astype(jnp.bfloat16)
    normed = normed_ref[...]
    ones = jnp.ones((8, 256), jnp.float32)
    for part in range(3):
        wide = jnp.dot(
            normed, w_ref[:, part * 256 : (part + 1) * 256], preferred_element_type=jnp.float32
        )
        narrow = wide.astype(jnp.bfloat16).reshape(Y, count, 256)
        mine_ref[:, :, part * 128 : (part + 1) * 128] = narrow[:, :, :128]
        other_ref[:, :, part * 128 : (part + 1) * 128] = narrow[:, :, 128:]
        if part < 2:
            for slot, offset in enumerate(OFFSETS):
                block = wide[slot * count : (slot + 1) * count]
                sums = lax.dot_general(
                    ones, block * block, (((1,), (1,)), ((), ())),
                    precision=lax.Precision.HIGHEST, preferred_element_type=jnp.float32,
                )
                target = lax.rem(place_ref[0] + (offset + Y), Y)
                power_ref[target, part : part + 1, :] = sums[:1]


def project(place, scale, shift, weights, pieces):
    count = pieces[0].shape[0]
    features = weights.shape[0]
    vmem = pl.BlockSpec(memory_space=pltpu.VMEM)
    return pl.pallas_call(
        project_kernel,
        out_shape=(
            jax.ShapeDtypeStruct((Y, count, 384), jnp.bfloat16),
            jax.ShapeDtypeStruct((Y, count, 384), jnp.bfloat16),
            jax.ShapeDtypeStruct((Y, 2, count), jnp.float32),
        ),
        in_specs=[pl.BlockSpec(memory_space=pltpu.SMEM)] + [vmem] * 8,
        out_specs=(vmem, vmem, vmem),
        scratch_shapes=[pltpu.VMEM((Y * count, features), jnp.bfloat16)],
        compiler_params=pltpu.CompilerParams(vmem_limit_bytes=40 * 2**20),
        cost_estimate=pl.CostEstimate(
            flops=2 * Y * count * features * 768, bytes_accessed=features * 1536 + Y * count * features * 2,
            transcendentals=0,
        ),
        name="project",
    )(place, scale, shift, weights, *pieces)


def attend_kernel(
    place_ref, power_ref, gain_ref, w_head_ref, own_ref, near_ref, far_ref,
    own_b_ref, near_b_ref, far_b_ref, out_ref, query0, query1, key, value, root,
):
    y_step, c_step = pl.program_id(0), pl.program_id(1)
    my_y, my_z = place_ref[0], place_ref[1]
    my_c = place_ref[2]
    all_cols = HD * 2 * Y * Z * C

    @pl.when((y_step == 0) & (c_step == 0))
    def _():
        totals = []
        for c in range(C):
            total = None
            for y in range(Y):
                for z in range(Z):
                    term = power_ref[(y * Z + z) * C + c]
                    total = term if total is None else total + term
            totals.append(lax.rsqrt(total / all_cols + 1e-6))
        first = lax.select(jnp.broadcast_to(my_c, (16, 128)) == 0, totals[0], totals[1])
        second = lax.select(jnp.broadcast_to(my_c, (16, 128)) == 0, totals[1], totals[0])
        root[0:16, :] = first
        root[16:32, :] = second
        columns = jnp.transpose(root[...])
        lane = lax.broadcasted_iota(jnp.int32, (128, 32), 1)
        head = lax.broadcasted_iota(jnp.int32, (1, 128), 1) < HD
        gain_q = gain_ref[0:1, :] * (HD ** (-0.5) * math.log2(math.e))
        gain_k = gain_ref[1:2, :]
        stacks = ((own_ref, near_ref, far_ref), (own_b_ref, near_b_ref, far_b_ref))
        for slot_c in range(C):
            for slot_y, offset in enumerate(OFFSETS):
                target = lax.rem(my_y + (offset + Y), Y)
                for slot_z in range(Z):
                    z_at = my_z if slot_z == 0 else 1 - my_z
                    at = target * Z + z_at + slot_c * 16
                    scale_q = jnp.sum(jnp.where(lane == at, columns, 0.0), axis=1, keepdims=True)
                    scale_k = jnp.sum(jnp.where(lane == at + 8, columns, 0.0), axis=1, keepdims=True)
                    base = ((slot_c * Y + slot_y) * Z + slot_z) * 128
                    if slot_z == 0:
                        parts = ((stacks[slot_c][0], 0, 128),)
                    else:
                        parts = tuple(
                            (ref, a, b) for ref, (a, b) in zip(stacks[slot_c][1:], CHUNKS)
                        )
                    for ref, a, b in parts:
                        span = slice(base + a, base + b)
                        query = ref[slot_y, :, 0:128].astype(jnp.float32) * scale_q[a:b] * gain_q
                        query0[span, :] = jnp.where(head, query, 0.0).astype(jnp.bfloat16)
                        query1[span, :] = jnp.where(head, 0.0, query).astype(jnp.bfloat16)
                        keys = ref[slot_y, :, 128:256].astype(jnp.float32) * scale_k[a:b] * gain_k
                        key[span, :] = keys.astype(jnp.bfloat16)
                        value[span, 0:128] = ref[slot_y, :, 256:384]
        value[:, 128:256] = jnp.ones((value.shape[0], 128), jnp.bfloat16)

    start = pl.multiple_of((c_step * Y + y_step) * 256, 256)
    outs = []
    for queries in (query0, query1):
        scores = lax.dot_general(
            queries[pl.ds(start, 256), :], key[...], (((1,), (1,)), ((), ())),
            preferred_element_type=jnp.float32,
        )
        highest = jnp.max(scores, axis=-1, keepdims=True)
        raised = jnp.exp2(scores - highest).astype(jnp.bfloat16)
        both = jnp.dot(raised, value[...], preferred_element_type=jnp.float32)
        outs.append(both[:, :128] / both[:, 128:])
    head = lax.broadcasted_iota(jnp.int32, (1, 128), 1) < HD
    attended = jnp.where(head, outs[0], outs[1]).astype(jnp.bfloat16)
    partial = jnp.dot(attended, w_head_ref[...], preferred_element_type=jnp.float32)
    partial = partial.astype(jnp.bfloat16)
    out_ref[0, my_z, 0] = partial[:128]
    out_ref[0, 1 - my_z, 0] = partial[128:]


def attend(place, powers, gains, w_head, mine, theirs):
    tokens = Y * Z * C * 128
    const = lambda rank: (lambda y, c, place: (0,) * rank)
    stack = [pl.BlockSpec(a.shape, const(3)) for a in (*mine, *theirs)]
    y_of = lambda y, place: lax.rem(
        place[0] + jnp.where(y == 0, 0, jnp.where(y == 1, Y - 1, jnp.where(y == 2, 1, 2))), Y
    )
    return pl.pallas_call(
        attend_kernel,
        out_shape=jax.ShapeDtypeStruct((Y, Z, C, 128, 64), jnp.bfloat16),
        grid_spec=pltpu.PrefetchScalarGridSpec(
            num_scalar_prefetch=1,
            grid=(Y, C),
            in_specs=[
                pl.BlockSpec(powers.shape, const(3)),
                pl.BlockSpec(gains.shape, const(2)),
                pl.BlockSpec((128, 64), lambda y, c, place: (place[3], 0)),
                *stack,
            ],
            out_specs=pl.BlockSpec(
                (1, Z, 1, 128, 64),
                lambda y, c, place: (y_of(y, place), 0, lax.rem(c + place[2], C), 0, 0),
            ),
            scratch_shapes=[
                pltpu.VMEM((tokens, 128), jnp.bfloat16),
                pltpu.VMEM((tokens, 128), jnp.bfloat16),
                pltpu.VMEM((tokens, 128), jnp.bfloat16),
                pltpu.VMEM((tokens, 256), jnp.bfloat16),
                pltpu.VMEM((32, 128), jnp.float32),
            ],
        ),
        compiler_params=pltpu.CompilerParams(vmem_limit_bytes=40 * 2**20),
        cost_estimate=pl.CostEstimate(
            flops=tokens * tokens * 1024, bytes_accessed=2**22, transcendentals=2 * tokens * tokens
        ),
        name="attend",
    )(place, powers, gains, w_head, *mine, *theirs)


def layer_norm(token_rows):
    average = jnp.mean(token_rows, axis=-1, keepdims=True)
    centred = token_rows - average
    spread = jnp.mean(centred * centred, axis=-1, keepdims=True)
    return centred * lax.rsqrt(spread + 1e-06)


def spread_over(value, axis, count, groups=None):
    copies = jnp.broadcast_to(value[None], (count,) + value.shape)
    return lax.all_to_all(copies, axis, 0, 0, axis_index_groups=groups)


def per_device(
    x_start, old_states, hidden, modulation, step_index, sigma_table,
    w_query, w_key, w_value, qk_gain, w_head, w_skip,
):
    seq_rank = lax.axis_index("seq").astype(jnp.int32)
    time_rank = lax.axis_index("tm").astype(jnp.int32)
    my_y, my_z, my_c = seq_rank // (Z * C), (seq_rank // C) % Z, seq_rank % C
    my_x, my_zl = time_rank // ZL, time_rank % ZL
    place = jnp.stack([my_y, my_z, my_c, seq_rank])
    raw = hidden[0]

    far = [lax.ppermute(raw[a:b], "seq", TO_FAR) for a, b in CHUNKS]

    w_mine = jnp.concatenate([w_query, w_key, w_value], axis=1)
    w_theirs = lax.ppermute(w_mine, "seq", TO_CORE)
    weights = jnp.concatenate(
        [w[:, i * 128 : (i + 1) * 128] for i in range(3) for w in (w_mine, w_theirs)], axis=1
    )
    following = jnp.concatenate([step_index[1:], step_index[-1:] + 1])
    step_now = lax.dynamic_index_in_dim(step_index, time_rank, 0, False)
    step_next = lax.dynamic_index_in_dim(following, time_rank, 0, False)
    delta = lax.dynamic_index_in_dim(sigma_table, step_next, 0, False) - (
        lax.dynamic_index_in_dim(sigma_table, step_now, 0, False)
    )
    mod_now = lax.dynamic_index_in_dim(modulation, step_now, 0, False)
    scale, shift = mod_now[0:1], mod_now[1:2]
    own_normed = (layer_norm(raw.astype(jnp.float32)) * (1.0 + scale) + shift).astype(jnp.bfloat16)
    skip = jnp.dot(own_normed, w_skip, preferred_element_type=jnp.float32)

    mine, theirs, powers = [], [], []
    for rows in (raw, *far):
        kept, given, power = project(place, scale, shift, weights, along_y(rows))
        mine.append(kept)
        theirs.append(lax.ppermute(given, "seq", TO_CORE))
        powers.append(power)
    power_own = powers[0]
    power_far = jnp.concatenate(powers[1:], axis=2)
    low = jnp.where(my_z == 0, power_own, power_far)
    high = jnp.where(my_z == 0, power_far, power_own)
    table = jnp.stack([low, high], axis=1).transpose(2, 0, 1, 3).reshape(2 * Y * Z, 128)
    powers = spread_over(table, "seq", Y * Z * C)

    partial = attend(place, powers, qk_gain, w_head, mine, theirs)
    partial = lax.all_to_all(partial.reshape(Y * Z * C, 128, 64), "seq", 0, 0)
    drift = jnp.sum(partial.astype(jnp.float32), axis=0) + skip

    increment = delta * drift
    z_groups = [[x * ZL + z for z in range(ZL)] for x in range(4)]
    x_groups = [[x * ZL + z for x in range(4)] for z in range(ZL)]
    line = spread_over(increment.astype(jnp.bfloat16), "tm", ZL, z_groups).astype(jnp.float32)
    total = jnp.sum(line, axis=0)
    before = (jnp.arange(ZL) < my_zl)[:, None, None]
    earlier = jnp.sum(jnp.where(before, line, 0.0), axis=0)
    totals = spread_over(total, "tm", 4, x_groups)
    before = (jnp.arange(4) < my_x)[:, None, None]
    earlier = earlier + jnp.sum(jnp.where(before, totals, 0.0), axis=0)
    new_state = x_start + (earlier + increment)
    change = new_state - old_states[0]
    square = jnp.sum(change * change)
    squares = spread_over(jnp.broadcast_to(square, (1, 128)), "seq", Y * Z * C)
    error = (jnp.sum(squares[:, 0, 0]) / (Y * Z * C * change.size)).reshape(1)
    return (drift[None], new_state[None], error)


def solution(mesh):
    return jax.shard_map(
        per_device,
        mesh=mesh,
        in_specs=(
            P("seq", None),
            P("tm", "seq", None),
            P("tm", "seq", None),
            P(),
            P(),
            P(),
            P(None, "seq"),
            P(None, "seq"),
            P(None, "seq"),
            P(None, "seq"),
            P(),
            P(),
        ),
        out_specs=(P("tm", "seq", None), P("tm", "seq", None), P("tm")),
        check_vma=False,
    )
```

```python
import functools
import math

import jax
import jax.numpy as jnp
from jax import lax
from jax.experimental import pallas as pl
from jax.experimental.pallas import tpu as pltpu
from jax.sharding import PartitionSpec as P

HD = 64
LAT = 64
Y, Z, C = 4, 2, 2
ZL = 8


Z_GROUPS = [
    [(x * ZL + zl) * Y * Z * C + (y * Z + z) * C + c for z in range(Z) for zl in range(ZL)]
    for x in range(4)
    for y in range(Y)
    for c in range(C)
]


def seq_perm(move):
    pairs = []
    for s in range(Y * Z * C):
        y, z, c = s // (Z * C), (s // C) % Z, s % C
        y, z, c = move(y, z, c)
        pairs.append((s, ((y % Y) * Z + z) * C + c))
    return pairs


TO_CORE = seq_perm(lambda y, z, c: (y, z, 1 - c))
Y_GROUPS = [[y * Z * C + r for y in range(Y)] for r in range(Z * C)]
YC_GROUPS = [[(y * Z + z) * C + c for y in range(Y) for c in range(C)] for z in range(Z)]
TO_UP = seq_perm(lambda y, z, c: (y + 1, z, c))
TO_DOWN = seq_perm(lambda y, z, c: (y - 1, z, c))
TO_FAR = seq_perm(lambda y, z, c: (y, 1 - z, c))


def along_y(rows):
    half = rows.shape[0] // 2
    below = lax.ppermute(rows, "seq", TO_UP)
    above = lax.ppermute(rows, "seq", TO_DOWN)
    return (
        rows, below, above,
        lax.ppermute(below[:half], "seq", TO_UP), lax.ppermute(above[half:], "seq", TO_DOWN),
    )


def project_kernel(
    order_ref, scale_ref, shift_ref, w_mine, w_theirs, rows_ref, mine_ref, other_ref, power_ref
):
    rows = rows_ref[...].astype(jnp.float32)
    average = jnp.mean(rows, axis=-1, keepdims=True)
    centred = rows - average
    spread = jnp.mean(centred * centred, axis=-1, keepdims=True)
    normed = centred * lax.rsqrt(spread + 1e-6) * (1.0 + scale_ref[...]) + shift_ref[...]
    normed = normed.astype(jnp.bfloat16)
    mine = jnp.dot(normed, w_mine[...], preferred_element_type=jnp.float32)
    other = jnp.dot(normed, w_theirs[...], preferred_element_type=jnp.float32)
    mine_ref[0] = mine
    other_ref[0] = other
    for part in range(2):
        cols = slice(part * 128, (part + 1) * 128)
        squares = mine[:, cols] * mine[:, cols] + other[:, cols] * other[:, cols]
        power_ref[0, part : part + 1, :] = jnp.sum(jnp.transpose(squares), axis=0, keepdims=True)


def project(order, scale, shift, w_mine, w_theirs, rows):
    features, columns = w_mine.shape
    count = rows.shape[0] // Y
    vmem = pl.BlockSpec(memory_space=pltpu.VMEM)
    stack = pl.BlockSpec((1, count, columns), lambda y, order: (order[y], 0, 0))
    return pl.pallas_call(
        project_kernel,
        out_shape=(
            jax.ShapeDtypeStruct((Y, count, columns), jnp.float32),
            jax.ShapeDtypeStruct((Y, count, columns), jnp.float32),
            jax.ShapeDtypeStruct((Y, 2, count), jnp.float32),
        ),
        grid_spec=pltpu.PrefetchScalarGridSpec(
            num_scalar_prefetch=1,
            grid=(Y,),
            in_specs=[vmem, vmem, vmem, vmem, pl.BlockSpec((count, features), lambda y, order: (y, 0))],
            out_specs=(stack, stack, pl.BlockSpec((1, 2, count), lambda y, order: (order[y], 0, 0))),
        ),
        compiler_params=pltpu.CompilerParams(vmem_limit_bytes=24 * 2**20),
        cost_estimate=pl.CostEstimate(
            flops=2 * Y * count * features * 768,
            bytes_accessed=features * 1536 + Y * count * features * 2,
            transcendentals=0,
        ),
        name="project",
    )(order, scale, shift, w_mine, w_theirs, rows)


def attend_kernel(chunks, place_ref, power_ref, gain_ref, w_head_ref, *refs):
    stacks = (refs[: len(chunks)], refs[len(chunks) : 2 * len(chunks)])
    out_ref, query0, query1, key0, key1, value, root = refs[2 * len(chunks) :]
    c_step = pl.program_id(0)
    my_z, my_c = place_ref[1], place_ref[2]
    all_cols = HD * 2 * Y * Z * C
    head = lax.broadcasted_iota(jnp.int32, (1, 128), 1) < HD

    @pl.when(c_step == 0)
    def _():
        totals = []
        for c in range(C):
            total = None
            for y in range(Y):
                for z in range(Z):
                    term = power_ref[(y * Z + z) * C + c]
                    total = term if total is None else total + term
            totals.append(lax.rsqrt(total / all_cols + 1e-6))
        flip = jnp.broadcast_to(my_c, (16, 128)) == 0
        root[0:16, :] = jnp.where(flip, totals[0], totals[1])
        root[16:32, :] = jnp.where(flip, totals[1], totals[0])
        columns = jnp.transpose(root[...])
        lane = lax.broadcasted_iota(jnp.int32, (128, 32), 1)
        gain_q = gain_ref[0:1, :]
        gain_k = gain_ref[1:2, :]
        for slot_c in range(C):
            for slot_y in range(Y):
                for slot_z in range(Z):
                    z_at = my_z if slot_z == 0 else 1 - my_z
                    at = slot_y * Z + z_at + slot_c * 16
                    scale_q = jnp.sum(jnp.where(lane == at, columns, 0.0), axis=1, keepdims=True)
                    scale_k = jnp.sum(jnp.where(lane == at + 8, columns, 0.0), axis=1, keepdims=True)
                    base = ((slot_c * Y + slot_y) * Z + slot_z) * 128
                    for ref, (kind, a, b) in zip(stacks[slot_c], chunks):
                        if kind != slot_z:
                            continue
                        span = slice(base + a, base + b)
                        unit = (ref[slot_y, :, 0:128] * scale_q[a:b] * gain_q).astype(jnp.bfloat16)
                        query = unit.astype(jnp.float32) * (HD ** (-0.5) * math.log2(math.e))
                        high = query.astype(jnp.bfloat16).astype(jnp.float32)
                        low = pltpu.roll(query - high, HD, 1)
                        query0[span, :] = jnp.where(head, high, low).astype(jnp.bfloat16)
                        query1[span, :] = jnp.where(head, low, high).astype(jnp.bfloat16)
                        keys = ref[slot_y, :, 128:256] * scale_k[a:b] * gain_k
                        turned = pltpu.roll(keys, HD, 1)
                        key0[span, :] = jnp.where(head, keys, turned).astype(jnp.bfloat16)
                        key1[span, :] = jnp.where(head, turned, keys).astype(jnp.bfloat16)
                        value[span, 0:128] = ref[slot_y, :, 256:384].astype(jnp.bfloat16)
        value[:, 128:256] = jnp.ones((value.shape[0], 128), jnp.bfloat16)

    count = Y * Z * 128
    start = pl.multiple_of(c_step * count, count)
    scores = [
        lax.dot_general(
            queries[pl.ds(start, count), :], keys[...], (((1,), (1,)), ((), ())),
            preferred_element_type=jnp.float32,
        )
        for queries, keys in ((query0, key0), (query1, key1))
    ]
    raised = [
        jnp.exp2(part - jnp.max(part, axis=-1, keepdims=True)).astype(jnp.bfloat16)
        for part in scores
    ]
    both = [jnp.dot(part, value[...], preferred_element_type=jnp.float32) for part in raised]
    outs = [part[:, :128] / part[:, 128:] for part in both]
    attended = jnp.where(head, outs[0], outs[1]).astype(jnp.bfloat16)
    partial = lax.dot_general(
        w_head_ref[...], attended, (((0,), (1,)), ((), ())), preferred_element_type=jnp.float32
    ).astype(jnp.bfloat16)
    for y in range(Y):
        at = y * Z * 128
        out_ref[y, 0, my_z] = partial[:, at : at + 128]
        out_ref[y, 0, 1 - my_z] = partial[:, at + 128 : at + 256]


def attend(chunks, place, powers, gains, w_head, mine, theirs):
    tokens = Y * Z * C * 128
    const = lambda rank: (lambda c, place: (0,) * rank)
    stack = [pl.BlockSpec(a.shape, const(3)) for a in (*mine, *theirs)]
    return pl.pallas_call(
        functools.partial(attend_kernel, chunks),
        out_shape=jax.ShapeDtypeStruct((Y, C, Z, 64, 128), jnp.bfloat16),
        grid_spec=pltpu.PrefetchScalarGridSpec(
            num_scalar_prefetch=1,
            grid=(C,),
            in_specs=[
                pl.BlockSpec(powers.shape, const(3)),
                pl.BlockSpec(gains.shape, const(2)),
                pl.BlockSpec((128, LAT), lambda c, place: (place[3], 0)),
                *stack,
            ],
            out_specs=pl.BlockSpec(
                (Y, 1, Z, LAT, 128),
                lambda c, place: (0, lax.rem(c + place[2], C), 0, 0, 0),
            ),
            scratch_shapes=[pltpu.VMEM((tokens, 128), jnp.bfloat16)] * 4
            + [pltpu.VMEM((tokens, 256), jnp.bfloat16), pltpu.VMEM((32, 128), jnp.float32)],
        ),
        compiler_params=pltpu.CompilerParams(vmem_limit_bytes=56 * 2**20),
        cost_estimate=pl.CostEstimate(
            flops=tokens * tokens * 1024, bytes_accessed=2**22, transcendentals=2 * tokens * tokens
        ),
        name="attend",
    )(place, powers, gains, w_head, *mine, *theirs)


def layer_norm(token_rows):
    average = jnp.mean(token_rows, axis=-1, keepdims=True)
    centred = token_rows - average
    spread = jnp.mean(centred * centred, axis=-1, keepdims=True)
    return centred * lax.rsqrt(spread + 1e-06)


def spread_over(value, axis, count, groups=None):
    copies = jnp.broadcast_to(value[None], (count,) + value.shape)
    return lax.all_to_all(copies, axis, 0, 0, axis_index_groups=groups)


def per_device(
    x_start, old_states, hidden, modulation, step_index, sigma_table,
    w_query, w_key, w_value, qk_gain, w_head, w_skip,
):
    seq_rank = lax.axis_index("seq").astype(jnp.int32)
    time_rank = lax.axis_index("tm").astype(jnp.int32)
    my_y, my_z, my_c = seq_rank // (Z * C), (seq_rank // C) % Z, seq_rank % C
    my_x, my_zl = time_rank // ZL, time_rank % ZL
    place = jnp.stack([my_y, my_z, my_c, seq_rank])
    raw = hidden[0]

    far = lax.ppermute(raw, "seq", TO_FAR)
    own = along_y(raw)
    w_parts, _ = lax.optimization_barrier(((w_query, w_key, w_value), own[1:3]))
    w_mine = jnp.concatenate(w_parts, axis=1)
    w_theirs = lax.ppermute(w_mine, "seq", TO_CORE)
    following = jnp.concatenate([step_index[1:], step_index[-1:] + 1])
    step_now = lax.dynamic_index_in_dim(step_index, time_rank, 0, False)
    step_next = lax.dynamic_index_in_dim(following, time_rank, 0, False)
    delta = lax.dynamic_index_in_dim(sigma_table, step_next, 0, False) - (
        lax.dynamic_index_in_dim(sigma_table, step_now, 0, False)
    )
    mod_now = lax.dynamic_index_in_dim(modulation, step_now, 0, False)
    scale, shift = mod_now[0:1], mod_now[1:2]
    own_normed = (layer_norm(raw.astype(jnp.float32)) * (1.0 + scale) + shift).astype(jnp.bfloat16)
    skip = jnp.dot(own_normed, w_skip, preferred_element_type=jnp.float32)

    mine, theirs, powers = [], [], []

    def project_stack(order, rows):
        kept, given, power = project(order, scale, shift, w_mine, w_theirs, rows)
        mine.append(kept)
        theirs.append(lax.ppermute(given, "seq", TO_CORE))
        powers.append(power)

    far, own = lax.optimization_barrier((far, own))
    far = spread_over(far, "seq", Y, Y_GROUPS).reshape(-1, raw.shape[1])
    project_stack(jnp.stack([my_y, my_y + 3, my_y + 1, my_y + 2]) % Y, jnp.concatenate(own))
    project_stack(jnp.arange(Y, dtype=jnp.int32), far)
    power_own, power_far = powers
    low = jnp.where(my_z == 0, power_own, power_far)
    high = jnp.where(my_z == 0, power_far, power_own)
    table = jnp.stack([low, high], axis=1).transpose(2, 0, 1, 3).reshape(2 * Y * Z, 128)
    powers = spread_over(table, "seq", Y * Z * C)

    chunks = ((0, 0, 128), (1, 0, 128))
    partial = attend(chunks, place, powers, qk_gain, w_head, mine, theirs)
    partial = partial.reshape(Y * C, Z, LAT, 128)
    partial = lax.all_to_all(partial, "seq", 0, 0, axis_index_groups=YC_GROUPS)
    partial = jnp.sum(partial.astype(jnp.float32), axis=0)
    here = lax.dynamic_index_in_dim(partial, my_z, 0, False) + skip.T
    owner = (jnp.arange(Z) == my_z)[:, None, None]
    sent = jnp.where(owner, here[None], partial).astype(jnp.bfloat16)
    sent = jnp.broadcast_to(sent[:, None], (Z, ZL, LAT, 128)).reshape(Z * ZL, LAT, 128)
    line = lax.all_to_all(sent, ("tm", "seq"), 0, 0, axis_index_groups=Z_GROUPS)
    line = line.reshape(Z, ZL, LAT, 128).astype(jnp.float32)
    there = lax.dynamic_index_in_dim(line, 1 - my_z, 0, False)
    drift = here + lax.dynamic_index_in_dim(there, my_zl, 0, False)
    increment = delta * drift
    steps = jnp.concatenate([step_index, step_index[-1:] + 1])
    sigmas = jnp.dot(
        (steps[:, None] == jnp.arange(sigma_table.shape[0])).astype(jnp.float32), sigma_table,
        precision=lax.Precision.HIGHEST,
    )
    deltas = lax.dynamic_slice_in_dim(sigmas[1:] - sigmas[:-1], my_x * ZL, ZL, 0)
    line = jnp.sum(line, axis=0) * deltas[:, None, None]
    total = jnp.sum(line, axis=0)
    before = (jnp.arange(ZL) < my_zl)[:, None, None]
    earlier = jnp.sum(jnp.where(before, line, 0.0), axis=0)
    x_groups = [[x * ZL + z for x in range(4)] for z in range(ZL)]
    totals = spread_over(total, "tm", 4, x_groups)
    before = (jnp.arange(4) < my_x)[:, None, None]
    earlier = earlier + jnp.sum(jnp.where(before, totals, 0.0), axis=0)
    new_state = x_start.T + (earlier + increment)
    change = new_state - old_states[0].T
    square = jnp.sum(change * change)
    squares = spread_over(jnp.broadcast_to(square, (1, 128)), "seq", Y * Z * C)
    error = (jnp.sum(squares[:, 0, 0]) / (Y * Z * C * change.size)).reshape(1)
    return (drift.T[None], new_state.T[None], error)


def solution(mesh):
    return jax.shard_map(
        per_device,
        mesh=mesh,
        in_specs=(
            P("seq", None),
            P("tm", "seq", None),
            P("tm", "seq", None),
            P(),
            P(),
            P(),
            P(None, "seq"),
            P(None, "seq"),
            P(None, "seq"),
            P(None, "seq"),
            P(),
            P(),
        ),
        out_specs=(P("tm", "seq", None), P("tm", "seq", None), P("tm")),
        check_vma=False,
    )
```

```python
import functools
import math

import jax
import jax.numpy as jnp
from jax import lax
from jax.experimental import pallas as pl
from jax.experimental.pallas import tpu as pltpu
from jax.sharding import PartitionSpec as P

HD = 64
LAT = 64
Y, Z, C = 4, 2, 2
ZL = 8


Z_GROUPS = [
    [(x * ZL + zl) * Y * Z * C + (y * Z + z) * C + c for z in range(Z) for zl in range(ZL)]
    for x in range(4)
    for y in range(Y)
    for c in range(C)
]


def seq_perm(move):
    pairs = []
    for s in range(Y * Z * C):
        y, z, c = s // (Z * C), (s // C) % Z, s % C
        y, z, c = move(y, z, c)
        pairs.append((s, ((y % Y) * Z + z) * C + c))
    return pairs


TO_CORE = seq_perm(lambda y, z, c: (y, z, 1 - c))
Y_GROUPS = [[y * Z * C + r for y in range(Y)] for r in range(Z * C)]
YC_GROUPS = [[(y * Z + z) * C + c for y in range(Y) for c in range(C)] for z in range(Z)]
CHUNKS = ((0, 128),)
TO_FAR = seq_perm(lambda y, z, c: (y, 1 - z, c))


def project_kernel(
    scale_ref, shift_ref, w_mine, w_theirs, rows_ref, mine_ref, other_ref, power_ref, normed_ref
):
    rows = rows_ref[...].astype(jnp.float32)
    average = jnp.mean(rows, axis=-1, keepdims=True)
    centred = rows - average
    spread = jnp.mean(centred * centred, axis=-1, keepdims=True)
    normed = centred * lax.rsqrt(spread + 1e-6) * (1.0 + scale_ref[...]) + shift_ref[...]
    normed_ref[...] = normed.astype(jnp.bfloat16)
    mine = jnp.dot(normed_ref[...], w_mine[...], preferred_element_type=jnp.float32)
    other = jnp.dot(normed_ref[...], w_theirs[...], preferred_element_type=jnp.float32)
    count = mine.shape[0] // Y
    for y in range(Y):
        rows = slice(y * count, (y + 1) * count)
        mine_ref[y] = mine[rows]
        other_ref[y] = other[rows]
        for part in range(2):
            cols = slice(part * 128, (part + 1) * 128)
            squares = mine[rows, cols] * mine[rows, cols] + other[rows, cols] * other[rows, cols]
            power_ref[y, part : part + 1, :] = jnp.sum(
                jnp.transpose(squares), axis=0, keepdims=True
            )


def project(scale, shift, w_mine, w_theirs, rows):
    features, columns = w_mine.shape
    count = rows.shape[0] // Y
    vmem = pl.BlockSpec(memory_space=pltpu.VMEM)
    return pl.pallas_call(
        project_kernel,
        out_shape=(
            jax.ShapeDtypeStruct((Y, count, columns), jnp.float32),
            jax.ShapeDtypeStruct((Y, count, columns), jnp.float32),
            jax.ShapeDtypeStruct((Y, 2, count), jnp.float32),
        ),
        in_specs=[vmem] * 5,
        out_specs=(vmem, vmem, vmem),
        scratch_shapes=[pltpu.VMEM(rows.shape, jnp.bfloat16)],
        compiler_params=pltpu.CompilerParams(vmem_limit_bytes=24 * 2**20),
        cost_estimate=pl.CostEstimate(
            flops=2 * Y * count * features * 768,
            bytes_accessed=features * 1536 + Y * count * features * 2,
            transcendentals=0,
        ),
        name="project",
    )(scale, shift, w_mine, w_theirs, rows)


def attend_kernel(chunks, place_ref, power_ref, gain_ref, w_head_ref, *refs):
    stacks = (refs[: len(chunks)], refs[len(chunks) : 2 * len(chunks)])
    out_ref, query0, query1, key0, key1, value, root = refs[2 * len(chunks) :]
    c_step = pl.program_id(0)
    my_z, my_c = place_ref[1], place_ref[2]
    all_cols = HD * 2 * Y * Z * C
    head = lax.broadcasted_iota(jnp.int32, (1, 128), 1) < HD

    @pl.when(c_step == 0)
    def _():
        totals = []
        for c in range(C):
            total = None
            for y in range(Y):
                for z in range(Z):
                    term = power_ref[(y * Z + z) * C + c]
                    total = term if total is None else total + term
            totals.append(lax.rsqrt(total / all_cols + 1e-6))
        flip = jnp.broadcast_to(my_c, (16, 128)) == 0
        root[0:16, :] = jnp.where(flip, totals[0], totals[1])
        root[16:32, :] = jnp.where(flip, totals[1], totals[0])
        columns = jnp.transpose(root[...])
        lane = lax.broadcasted_iota(jnp.int32, (128, 32), 1)
        gain_q = gain_ref[0:1, :]
        gain_k = gain_ref[1:2, :]
        for slot_c in range(C):
            for slot_y in range(Y):
                for slot_z in range(Z):
                    z_at = my_z if slot_z == 0 else 1 - my_z
                    at = slot_y * Z + z_at + slot_c * 16
                    scale_q = jnp.sum(jnp.where(lane == at, columns, 0.0), axis=1, keepdims=True)
                    scale_k = jnp.sum(jnp.where(lane == at + 8, columns, 0.0), axis=1, keepdims=True)
                    base = ((slot_c * Y + slot_y) * Z + slot_z) * 128
                    for ref, (kind, a, b) in zip(stacks[slot_c], chunks):
                        if kind != slot_z:
                            continue
                        span = slice(base + a, base + b)
                        unit = (ref[slot_y, :, 0:128] * scale_q[a:b] * gain_q).astype(jnp.bfloat16)
                        query = unit.astype(jnp.float32) * (HD ** (-0.5) * math.log2(math.e))
                        high = query.astype(jnp.bfloat16).astype(jnp.float32)
                        low = pltpu.roll(query - high, HD, 1)
                        query0[span, :] = jnp.where(head, high, low).astype(jnp.bfloat16)
                        query1[span, :] = jnp.where(head, low, high).astype(jnp.bfloat16)
                        keys = ref[slot_y, :, 128:256] * scale_k[a:b] * gain_k
                        turned = pltpu.roll(keys, HD, 1)
                        key0[span, :] = jnp.where(head, keys, turned).astype(jnp.bfloat16)
                        key1[span, :] = jnp.where(head, turned, keys).astype(jnp.bfloat16)
                        value[span, 0:128] = ref[slot_y, :, 256:384].astype(jnp.bfloat16)
        value[:, 128:256] = jnp.ones((value.shape[0], 128), jnp.bfloat16)

    count = Y * Z * 128
    start = pl.multiple_of(c_step * count, count)
    scores = [
        lax.dot_general(
            queries[pl.ds(start, count), :], keys[...], (((1,), (1,)), ((), ())),
            preferred_element_type=jnp.float32,
        )
        for queries, keys in ((query0, key0), (query1, key1))
    ]
    raised = [
        jnp.exp2(part - jnp.max(part, axis=-1, keepdims=True)).astype(jnp.bfloat16)
        for part in scores
    ]
    both = [jnp.dot(part, value[...], preferred_element_type=jnp.float32) for part in raised]
    outs = [part[:, :128] / part[:, 128:] for part in both]
    attended = jnp.where(head, outs[0], outs[1]).astype(jnp.bfloat16)
    partial = lax.dot_general(
        w_head_ref[...], attended, (((0,), (1,)), ((), ())), preferred_element_type=jnp.float32
    ).astype(jnp.bfloat16)
    for y in range(Y):
        at = y * Z * 128
        out_ref[y, 0, my_z] = partial[:, at : at + 128]
        out_ref[y, 0, 1 - my_z] = partial[:, at + 128 : at + 256]


def attend(chunks, place, powers, gains, w_head, mine, theirs):
    tokens = Y * Z * C * 128
    const = lambda rank: (lambda c, place: (0,) * rank)
    stack = [pl.BlockSpec(a.shape, const(3)) for a in (*mine, *theirs)]
    return pl.pallas_call(
        functools.partial(attend_kernel, chunks),
        out_shape=jax.ShapeDtypeStruct((Y, C, Z, 64, 128), jnp.bfloat16),
        grid_spec=pltpu.PrefetchScalarGridSpec(
            num_scalar_prefetch=1,
            grid=(C,),
            in_specs=[
                pl.BlockSpec(powers.shape, const(3)),
                pl.BlockSpec(gains.shape, const(2)),
                pl.BlockSpec((128, LAT), lambda c, place: (place[3], 0)),
                *stack,
            ],
            out_specs=pl.BlockSpec(
                (Y, 1, Z, LAT, 128),
                lambda c, place: (0, lax.rem(c + place[2], C), 0, 0, 0),
            ),
            scratch_shapes=[pltpu.VMEM((tokens, 128), jnp.bfloat16)] * 4
            + [pltpu.VMEM((tokens, 256), jnp.bfloat16), pltpu.VMEM((32, 128), jnp.float32)],
        ),
        compiler_params=pltpu.CompilerParams(vmem_limit_bytes=56 * 2**20),
        cost_estimate=pl.CostEstimate(
            flops=tokens * tokens * 1024, bytes_accessed=2**22, transcendentals=2 * tokens * tokens
        ),
        name="attend",
    )(place, powers, gains, w_head, *mine, *theirs)


def layer_norm(token_rows):
    average = jnp.mean(token_rows, axis=-1, keepdims=True)
    centred = token_rows - average
    spread = jnp.mean(centred * centred, axis=-1, keepdims=True)
    return centred * lax.rsqrt(spread + 1e-06)


def spread_over(value, axis, count, groups=None):
    copies = jnp.broadcast_to(value[None], (count,) + value.shape)
    return lax.all_to_all(copies, axis, 0, 0, axis_index_groups=groups)


def per_device(
    x_start, old_states, hidden, modulation, step_index, sigma_table,
    w_query, w_key, w_value, qk_gain, w_head, w_skip,
):
    seq_rank = lax.axis_index("seq").astype(jnp.int32)
    time_rank = lax.axis_index("tm").astype(jnp.int32)
    my_y, my_z, my_c = seq_rank // (Z * C), (seq_rank // C) % Z, seq_rank % C
    my_x, my_zl = time_rank // ZL, time_rank % ZL
    place = jnp.stack([my_y, my_z, my_c, seq_rank])
    raw = hidden[0]

    far = [lax.ppermute(raw[a:b], "seq", TO_FAR) for a, b in CHUNKS]

    once = lax.optimization_barrier(jnp.int32(1))
    own = lax.fori_loop(
        0, once, lambda _, own: spread_over(raw, "seq", Y, Y_GROUPS), jnp.zeros((Y,) + raw.shape, raw.dtype)
    )
    parts, own = lax.optimization_barrier(((w_query, w_key, w_value), own))
    w_mine = jnp.concatenate(parts, axis=1)
    w_theirs = lax.ppermute(w_mine, "seq", TO_CORE)
    own = own.reshape(-1, raw.shape[1])
    following = jnp.concatenate([step_index[1:], step_index[-1:] + 1])
    step_now = lax.dynamic_index_in_dim(step_index, time_rank, 0, False)
    step_next = lax.dynamic_index_in_dim(following, time_rank, 0, False)
    delta = lax.dynamic_index_in_dim(sigma_table, step_next, 0, False) - (
        lax.dynamic_index_in_dim(sigma_table, step_now, 0, False)
    )
    mod_now = lax.dynamic_index_in_dim(modulation, step_now, 0, False)
    scale, shift = mod_now[0:1], mod_now[1:2]
    own_normed = (layer_norm(raw.astype(jnp.float32)) * (1.0 + scale) + shift).astype(jnp.bfloat16)
    skip = jnp.dot(own_normed, w_skip, preferred_element_type=jnp.float32)

    mine, theirs, powers = [], [], []

    def project_stack(rows):
        kept, given, power = project(scale, shift, w_mine, w_theirs, rows)
        mine.append(kept)
        theirs.append(lax.ppermute(given, "seq", TO_CORE))
        powers.append(power)

    project_stack(own)
    for at, rows in enumerate(far):
        if at > 0:
            rows, stack = lax.optimization_barrier((rows, stack))
            project_stack(stack)
        else:
            rows, _ = lax.optimization_barrier((rows, own))
        stack = spread_over(rows, "seq", Y, Y_GROUPS).reshape(-1, raw.shape[1])
    stack, _ = lax.optimization_barrier((stack, powers))
    project_stack(stack)
    power_own, power_far = powers[0], jnp.concatenate(powers[1:], axis=2)
    low = jnp.where(my_z == 0, power_own, power_far)
    high = jnp.where(my_z == 0, power_far, power_own)
    table = jnp.stack([low, high], axis=1).transpose(2, 0, 1, 3).reshape(2 * Y * Z, 128)
    powers = spread_over(table, "seq", Y * Z * C)

    chunks = ((0, 0, 128),) + tuple((1, a, b) for a, b in CHUNKS)
    partial = attend(chunks, place, powers, qk_gain, w_head, mine, theirs)
    partial = partial.reshape(Y * C, Z, LAT, 128)
    partial = lax.all_to_all(partial, "seq", 0, 0, axis_index_groups=YC_GROUPS)
    partial = jnp.sum(partial.astype(jnp.float32), axis=0)
    here = lax.dynamic_index_in_dim(partial, my_z, 0, False) + skip.T
    owner = (jnp.arange(Z) == my_z)[:, None, None]
    sent = jnp.where(owner, here[None], partial).astype(jnp.bfloat16)
    sent = jnp.broadcast_to(sent[:, None], (Z, ZL, LAT, 128)).reshape(Z * ZL, LAT, 128)
    line = lax.all_to_all(sent, ("tm", "seq"), 0, 0, axis_index_groups=Z_GROUPS)
    line = line.reshape(Z, ZL, LAT, 128).astype(jnp.float32)
    there = lax.dynamic_index_in_dim(line, 1 - my_z, 0, False)
    drift = here + lax.dynamic_index_in_dim(there, my_zl, 0, False)
    increment = delta * drift
    steps = jnp.concatenate([step_index, step_index[-1:] + 1])
    sigmas = jnp.dot(
        (steps[:, None] == jnp.arange(sigma_table.shape[0])).astype(jnp.float32), sigma_table,
        precision=lax.Precision.HIGHEST,
    )
    deltas = lax.dynamic_slice_in_dim(sigmas[1:] - sigmas[:-1], my_x * ZL, ZL, 0)
    line = jnp.sum(line, axis=0) * deltas[:, None, None]
    total = jnp.sum(line, axis=0)
    before = (jnp.arange(ZL) < my_zl)[:, None, None]
    earlier = jnp.sum(jnp.where(before, line, 0.0), axis=0)
    x_groups = [[x * ZL + z for x in range(4)] for z in range(ZL)]
    totals = spread_over(total, "tm", 4, x_groups)
    before = (jnp.arange(4) < my_x)[:, None, None]
    earlier = earlier + jnp.sum(jnp.where(before, totals, 0.0), axis=0)
    new_state = x_start.T + (earlier + increment)
    change = new_state - old_states[0].T
    square = jnp.sum(change * change)
    squares = spread_over(jnp.broadcast_to(square, (1, 128)), "seq", Y * Z * C)
    error = (jnp.sum(squares[:, 0, 0]) / (Y * Z * C * change.size)).reshape(1)
    return (drift.T[None], new_state.T[None], error)


def solution(mesh):
    return jax.shard_map(
        per_device,
        mesh=mesh,
        in_specs=(
            P("seq", None),
            P("tm", "seq", None),
            P("tm", "seq", None),
            P(),
            P(),
            P(),
            P(None, "seq"),
            P(None, "seq"),
            P(None, "seq"),
            P(None, "seq"),
            P(),
            P(),
        ),
        out_specs=(P("tm", "seq", None), P("tm", "seq", None), P("tm")),
        check_vma=False,
    )
```

```python
import functools
import math

import jax
import jax.numpy as jnp
from jax import lax
from jax.experimental import pallas as pl
from jax.experimental.pallas import tpu as pltpu
from jax.sharding import PartitionSpec as P

HD = 64
LAT = 64
Y, Z, C = 4, 2, 2
ZL = 8


Z_GROUPS = [
    [(x * ZL + zl) * Y * Z * C + (y * Z + z) * C + c for z in range(Z) for zl in range(ZL)]
    for x in range(4)
    for y in range(Y)
    for c in range(C)
]

TO_ACROSS = [(t, t // ZL * ZL + (t + ZL // 2) % ZL) for t in range(4 * ZL)]
ERROR_GROUPS = [
    [
        (x * ZL + (z_lo + z * ZL // 2) % ZL) * Y * Z * C + (y * Z + z) * C + c
        for z in range(Z)
        for y in range(Y)
        for c in range(C)
    ]
    for x in range(4)
    for z_lo in range(ZL)
]


def seq_perm(move):
    pairs = []
    for s in range(Y * Z * C):
        y, z, c = s // (Z * C), (s // C) % Z, s % C
        y, z, c = move(y, z, c)
        pairs.append((s, ((y % Y) * Z + z) * C + c))
    return pairs


TO_CORE = seq_perm(lambda y, z, c: (y, z, 1 - c))
Y_GROUPS = [[y * Z * C + r for y in range(Y)] for r in range(Z * C)]
YC_GROUPS = [[(y * Z + z) * C + c for y in range(Y) for c in range(C)] for z in range(Z)]
CHUNKS = ((0, 128),)
TO_FAR = seq_perm(lambda y, z, c: (y, 1 - z, c))


def project_kernel(
    scale_ref, shift_ref, w_mine, w_theirs, rows_ref, mine_ref, other_ref, power_ref, normed_ref
):
    rows = rows_ref[...].astype(jnp.float32)
    average = jnp.mean(rows, axis=-1, keepdims=True)
    centred = rows - average
    spread = jnp.mean(centred * centred, axis=-1, keepdims=True)
    normed = centred * lax.rsqrt(spread + 1e-6) * (1.0 + scale_ref[...]) + shift_ref[...]
    normed_ref[...] = normed.astype(jnp.bfloat16)
    mine = jnp.dot(normed_ref[...], w_mine[...], preferred_element_type=jnp.float32)
    other = jnp.dot(normed_ref[...], w_theirs[...], preferred_element_type=jnp.float32)
    count = mine.shape[0] // Y
    for y in range(Y):
        rows = slice(y * count, (y + 1) * count)
        mine_ref[y] = mine[rows]
        other_ref[y] = other[rows]
        for part in range(2):
            cols = slice(part * 128, (part + 1) * 128)
            squares = mine[rows, cols] * mine[rows, cols] + other[rows, cols] * other[rows, cols]
            power_ref[y, part : part + 1, :] = jnp.sum(
                jnp.transpose(squares), axis=0, keepdims=True
            )


def project(scale, shift, w_mine, w_theirs, rows):
    features, columns = w_mine.shape
    count = rows.shape[0] // Y
    vmem = pl.BlockSpec(memory_space=pltpu.VMEM)
    return pl.pallas_call(
        project_kernel,
        out_shape=(
            jax.ShapeDtypeStruct((Y, count, columns), jnp.float32),
            jax.ShapeDtypeStruct((Y, count, columns), jnp.float32),
            jax.ShapeDtypeStruct((Y, 2, count), jnp.float32),
        ),
        in_specs=[vmem] * 5,
        out_specs=(vmem, vmem, vmem),
        scratch_shapes=[pltpu.VMEM(rows.shape, jnp.bfloat16)],
        compiler_params=pltpu.CompilerParams(vmem_limit_bytes=24 * 2**20),
        cost_estimate=pl.CostEstimate(
            flops=2 * Y * count * features * 768,
            bytes_accessed=features * 1536 + Y * count * features * 2,
            transcendentals=0,
        ),
        name="project",
    )(scale, shift, w_mine, w_theirs, rows)


def attend_kernel(chunks, place_ref, power_ref, gain_ref, w_head_ref, *refs):
    stacks = (refs[: len(chunks)], refs[len(chunks) : 2 * len(chunks)])
    out_ref, query0, query1, key0, key1, value, root = refs[2 * len(chunks) :]
    c_step = pl.program_id(0)
    my_z, my_c = place_ref[1], place_ref[2]
    all_cols = HD * 2 * Y * Z * C
    head = lax.broadcasted_iota(jnp.int32, (1, 128), 1) < HD

    @pl.when(c_step == 0)
    def _():
        totals = []
        for c in range(C):
            total = None
            for y in range(Y):
                for z in range(Z):
                    term = power_ref[(y * Z + z) * C + c]
                    total = term if total is None else total + term
            totals.append(lax.rsqrt(total / all_cols + 1e-6))
        flip = jnp.broadcast_to(my_c, (16, 128)) == 0
        root[0:16, :] = jnp.where(flip, totals[0], totals[1])
        root[16:32, :] = jnp.where(flip, totals[1], totals[0])
        columns = jnp.transpose(root[...])
        lane = lax.broadcasted_iota(jnp.int32, (128, 32), 1)
        gain_q = gain_ref[0:1, :]
        gain_k = gain_ref[1:2, :]
        for slot_c in range(C):
            for slot_y in range(Y):
                for slot_z in range(Z):
                    z_at = my_z if slot_z == 0 else 1 - my_z
                    at = slot_y * Z + z_at + slot_c * 16
                    scale_q = jnp.sum(jnp.where(lane == at, columns, 0.0), axis=1, keepdims=True)
                    scale_k = jnp.sum(jnp.where(lane == at + 8, columns, 0.0), axis=1, keepdims=True)
                    base = ((slot_c * Y + slot_y) * Z + slot_z) * 128
                    for ref, (kind, a, b) in zip(stacks[slot_c], chunks):
                        if kind != slot_z:
                            continue
                        span = slice(base + a, base + b)
                        unit = (ref[slot_y, :, 0:128] * scale_q[a:b] * gain_q).astype(jnp.bfloat16)
                        query = unit.astype(jnp.float32) * (HD ** (-0.5) * math.log2(math.e))
                        high = query.astype(jnp.bfloat16).astype(jnp.float32)
                        low = pltpu.roll(query - high, HD, 1)
                        query0[span, :] = jnp.where(head, high, low).astype(jnp.bfloat16)
                        query1[span, :] = jnp.where(head, low, high).astype(jnp.bfloat16)
                        keys = ref[slot_y, :, 128:256] * scale_k[a:b] * gain_k
                        turned = pltpu.roll(keys, HD, 1)
                        key0[span, :] = jnp.where(head, keys, turned).astype(jnp.bfloat16)
                        key1[span, :] = jnp.where(head, turned, keys).astype(jnp.bfloat16)
                        value[span, 0:128] = ref[slot_y, :, 256:384].astype(jnp.bfloat16)
        value[:, 128:256] = jnp.ones((value.shape[0], 128), jnp.bfloat16)

    count = Y * Z * 128
    start = pl.multiple_of(c_step * count, count)
    scores = [
        lax.dot_general(
            queries[pl.ds(start, count), :], keys[...], (((1,), (1,)), ((), ())),
            preferred_element_type=jnp.float32,
        )
        for queries, keys in ((query0, key0), (query1, key1))
    ]
    raised = [
        jnp.exp2(part - jnp.max(part, axis=-1, keepdims=True)).astype(jnp.bfloat16)
        for part in scores
    ]
    both = [jnp.dot(part, value[...], preferred_element_type=jnp.float32) for part in raised]
    outs = [part[:, :128] / part[:, 128:] for part in both]
    attended = jnp.where(head, outs[0], outs[1]).astype(jnp.bfloat16)
    partial = lax.dot_general(
        w_head_ref[...], attended, (((0,), (1,)), ((), ())), preferred_element_type=jnp.float32
    ).astype(jnp.bfloat16)
    for y in range(Y):
        at = y * Z * 128
        out_ref[y, 0, my_z] = partial[:, at : at + 128]
        out_ref[y, 0, 1 - my_z] = partial[:, at + 128 : at + 256]


def attend(chunks, place, powers, gains, w_head, mine, theirs):
    tokens = Y * Z * C * 128
    const = lambda rank: (lambda c, place: (0,) * rank)
    stack = [pl.BlockSpec(a.shape, const(3)) for a in (*mine, *theirs)]
    return pl.pallas_call(
        functools.partial(attend_kernel, chunks),
        out_shape=jax.ShapeDtypeStruct((Y, C, Z, 64, 128), jnp.bfloat16),
        grid_spec=pltpu.PrefetchScalarGridSpec(
            num_scalar_prefetch=1,
            grid=(C,),
            in_specs=[
                pl.BlockSpec(powers.shape, const(3)),
                pl.BlockSpec(gains.shape, const(2)),
                pl.BlockSpec((128, LAT), lambda c, place: (place[3], 0)),
                *stack,
            ],
            out_specs=pl.BlockSpec(
                (Y, 1, Z, LAT, 128),
                lambda c, place: (0, lax.rem(c + place[2], C), 0, 0, 0),
            ),
            scratch_shapes=[pltpu.VMEM((tokens, 128), jnp.bfloat16)] * 4
            + [pltpu.VMEM((tokens, 256), jnp.bfloat16), pltpu.VMEM((32, 128), jnp.float32)],
        ),
        compiler_params=pltpu.CompilerParams(vmem_limit_bytes=56 * 2**20),
        cost_estimate=pl.CostEstimate(
            flops=tokens * tokens * 1024, bytes_accessed=2**22, transcendentals=2 * tokens * tokens
        ),
        name="attend",
    )(place, powers, gains, w_head, *mine, *theirs)


def layer_norm(token_rows):
    average = jnp.mean(token_rows, axis=-1, keepdims=True)
    centred = token_rows - average
    spread = jnp.mean(centred * centred, axis=-1, keepdims=True)
    return centred * lax.rsqrt(spread + 1e-06)


def spread_over(value, axis, count, groups=None):
    copies = jnp.broadcast_to(value[None], (count,) + value.shape)
    return lax.all_to_all(copies, axis, 0, 0, axis_index_groups=groups)


def per_device(
    x_start, old_states, hidden, modulation, step_index, sigma_table,
    w_query, w_key, w_value, qk_gain, w_head, w_skip,
):
    seq_rank = lax.axis_index("seq").astype(jnp.int32)
    time_rank = lax.axis_index("tm").astype(jnp.int32)
    my_y, my_z, my_c = seq_rank // (Z * C), (seq_rank // C) % Z, seq_rank % C
    my_x, my_zl = time_rank // ZL, time_rank % ZL
    place = jnp.stack([my_y, my_z, my_c, seq_rank])
    raw = hidden[0]

    far = [lax.ppermute(raw[a:b], "seq", TO_FAR) for a, b in CHUNKS]

    once = lax.optimization_barrier(jnp.int32(1))
    own = lax.fori_loop(
        0, once, lambda _, own: spread_over(raw, "seq", Y, Y_GROUPS), jnp.zeros((Y,) + raw.shape, raw.dtype)
    )
    parts, own = lax.optimization_barrier(((w_query, w_key, w_value), own))
    w_mine = jnp.concatenate(parts, axis=1)
    w_theirs = lax.ppermute(w_mine, "seq", TO_CORE)
    own = own.reshape(-1, raw.shape[1])
    following = jnp.concatenate([step_index[1:], step_index[-1:] + 1])
    step_now = lax.dynamic_index_in_dim(step_index, time_rank, 0, False)
    step_next = lax.dynamic_index_in_dim(following, time_rank, 0, False)
    delta = lax.dynamic_index_in_dim(sigma_table, step_next, 0, False) - (
        lax.dynamic_index_in_dim(sigma_table, step_now, 0, False)
    )
    mod_now = lax.dynamic_index_in_dim(modulation, step_now, 0, False)
    scale, shift = mod_now[0:1], mod_now[1:2]
    own_normed = (layer_norm(raw.astype(jnp.float32)) * (1.0 + scale) + shift).astype(jnp.bfloat16)
    skip = jnp.dot(own_normed, w_skip, preferred_element_type=jnp.float32)

    mine, theirs, powers = [], [], []

    def project_stack(rows):
        kept, given, power = project(scale, shift, w_mine, w_theirs, rows)
        mine.append(kept)
        theirs.append(lax.ppermute(given, "seq", TO_CORE))
        powers.append(power)

    project_stack(own)
    old_here, own_power = lax.optimization_barrier((old_states[0], powers[0]))
    powers[0] = own_power
    old_there = lax.ppermute(old_here, "tm", TO_ACROSS)
    rows, _ = lax.optimization_barrier((far[0], own))
    stack = spread_over(rows, "seq", Y, Y_GROUPS).reshape(-1, raw.shape[1])
    stack, old_there = lax.optimization_barrier((stack, old_there))
    project_stack(stack)
    power_own, power_far = powers
    low = jnp.where(my_z == 0, power_own, power_far)
    high = jnp.where(my_z == 0, power_far, power_own)
    table = jnp.stack([low, high], axis=1).transpose(2, 0, 1, 3).reshape(2 * Y * Z, 128)
    powers = spread_over(table, "seq", Y * Z * C)

    chunks = ((0, 0, 128),) + tuple((1, a, b) for a, b in CHUNKS)
    partial = attend(chunks, place, powers, qk_gain, w_head, mine, theirs)
    partial = partial.reshape(Y * C, Z, LAT, 128)
    partial = lax.all_to_all(partial, "seq", 0, 0, axis_index_groups=YC_GROUPS)
    partial = jnp.sum(partial.astype(jnp.float32), axis=0)
    here = lax.dynamic_index_in_dim(partial, my_z, 0, False) + skip.T
    owner = (jnp.arange(Z) == my_z)[:, None, None]
    sent = jnp.where(owner, here[None], partial).astype(jnp.bfloat16)
    sent = jnp.broadcast_to(sent[:, None], (Z, ZL, LAT, 128)).reshape(Z * ZL, LAT, 128)
    line = lax.all_to_all(sent, ("tm", "seq"), 0, 0, axis_index_groups=Z_GROUPS)
    line = line.reshape(Z, ZL, LAT, 128).astype(jnp.float32)
    there = lax.dynamic_index_in_dim(line, 1 - my_z, 0, False)
    drift = here + lax.dynamic_index_in_dim(there, my_zl, 0, False)
    increment = delta * drift
    steps = jnp.concatenate([step_index, step_index[-1:] + 1])
    sigmas = jnp.dot(
        (steps[:, None] == jnp.arange(sigma_table.shape[0])).astype(jnp.float32), sigma_table,
        precision=lax.Precision.HIGHEST,
    )
    deltas = lax.dynamic_slice_in_dim(sigmas[1:] - sigmas[:-1], my_x * ZL, ZL, 0)
    line = jnp.sum(line, axis=0) * deltas[:, None, None]
    total = jnp.sum(line, axis=0)
    before = (jnp.arange(ZL) < my_zl)[:, None, None]
    earlier = jnp.sum(jnp.where(before, line, 0.0), axis=0)
    x_groups = [[x * ZL + z for x in range(4)] for z in range(ZL)]
    totals = spread_over(total, "tm", 4, x_groups)
    before = (jnp.arange(4) < my_x)[:, None, None]
    entered = jnp.sum(jnp.where(before, totals, 0.0), axis=0) + x_start.T
    new_state = entered + (earlier + increment)
    change = new_state - old_states[0].T
    square = jnp.sum(change * change)
    upto = (jnp.arange(ZL) <= (my_zl + ZL // 2) % ZL)[:, None, None]
    change_there = entered + jnp.sum(jnp.where(upto, line, 0.0), axis=0) - old_there.T
    square_there = jnp.sum(change_there * change_there)
    squares = jnp.where(jnp.arange(Z) == my_z, square, square_there)
    squares = jnp.broadcast_to(squares[:, None, None, None], (Z, Y * C, 1, 128))
    squares = lax.all_to_all(
        squares.reshape(Z * Y * C, 1, 128), ("tm", "seq"), 0, 0, axis_index_groups=ERROR_GROUPS
    )
    error = (jnp.sum(squares[:, 0, 0]) / (Y * Z * C * change.size)).reshape(1)
    return (drift.T[None], new_state.T[None], error)


def solution(mesh):
    return jax.shard_map(
        per_device,
        mesh=mesh,
        in_specs=(
            P("seq", None),
            P("tm", "seq", None),
            P("tm", "seq", None),
            P(),
            P(),
            P(),
            P(None, "seq"),
            P(None, "seq"),
            P(None, "seq"),
            P(None, "seq"),
            P(),
            P(),
        ),
        out_specs=(P("tm", "seq", None), P("tm", "seq", None), P("tm")),
        check_vma=False,
    )
```

```python
import functools
import math

import jax
import jax.numpy as jnp
from jax import lax
from jax.experimental import pallas as pl
from jax.experimental.pallas import tpu as pltpu
from jax.sharding import PartitionSpec as P

HD = 64
LAT = 64
Y, Z, C = 4, 2, 2
ZL = 8


Z_GROUPS = [
    [(x * ZL + zl) * Y * Z * C + (y * Z + z) * C + c for z in range(Z) for zl in range(ZL)]
    for x in range(4)
    for y in range(Y)
    for c in range(C)
]

TO_ACROSS = [(t, t // ZL * ZL + (t + ZL // 2) % ZL) for t in range(4 * ZL)]
ERROR_GROUPS = [
    [
        (x * ZL + (z_lo + z * ZL // 2) % ZL) * Y * Z * C + (y * Z + z) * C + c
        for z in range(Z)
        for y in range(Y)
        for c in range(C)
    ]
    for x in range(4)
    for z_lo in range(ZL)
]


def seq_perm(move):
    pairs = []
    for s in range(Y * Z * C):
        y, z, c = s // (Z * C), (s // C) % Z, s % C
        y, z, c = move(y, z, c)
        pairs.append((s, ((y % Y) * Z + z) * C + c))
    return pairs


TO_CORE = seq_perm(lambda y, z, c: (y, z, 1 - c))
Y_GROUPS = [[y * Z * C + r for y in range(Y)] for r in range(Z * C)]
YC_GROUPS = [[(y * Z + z) * C + c for y in range(Y) for c in range(C)] for z in range(Z)]
CHUNKS = ((0, 128),)
TO_FAR = seq_perm(lambda y, z, c: (y, 1 - z, c))


def project_kernel(scale_ref, shift_ref, w_mine, w_theirs, rows_ref, *refs):
    power_ref, normed_ref = refs[-2:]
    mine_refs, other_refs = refs[: len(refs) // 2 - 1], refs[len(refs) // 2 - 1 : -2]
    rows = rows_ref[...].astype(jnp.float32)
    average = jnp.mean(rows, axis=-1, keepdims=True)
    centred = rows - average
    spread = jnp.mean(centred * centred, axis=-1, keepdims=True)
    normed = centred * lax.rsqrt(spread + 1e-6) * (1.0 + scale_ref[...]) + shift_ref[...]
    normed_ref[...] = normed.astype(jnp.bfloat16)
    mine = jnp.dot(normed_ref[...], w_mine[...], preferred_element_type=jnp.float32)
    other = jnp.dot(normed_ref[...], w_theirs[...], preferred_element_type=jnp.float32)
    count = mine.shape[0] // Y
    for y in range(Y):
        rows = slice(y * count, (y + 1) * count)
        for outs, wide in ((mine_refs, mine), (other_refs, other)):
            size = count // len(outs)
            for at, out in enumerate(outs):
                out[y] = wide[y * count + at * size : y * count + (at + 1) * size]
        for part in range(2):
            cols = slice(part * 128, (part + 1) * 128)
            squares = mine[rows, cols] * mine[rows, cols] + other[rows, cols] * other[rows, cols]
            power_ref[y, part : part + 1, :] = jnp.sum(
                jnp.transpose(squares), axis=0, keepdims=True
            )


def project(scale, shift, w_mine, w_theirs, rows, cuts):
    features, columns = w_mine.shape
    count = rows.shape[0] // Y
    vmem = pl.BlockSpec(memory_space=pltpu.VMEM)
    stack = jax.ShapeDtypeStruct((Y, count // cuts, columns), jnp.float32)
    outs = pl.pallas_call(
        project_kernel,
        out_shape=(stack,) * (2 * cuts) + (jax.ShapeDtypeStruct((Y, 2, count), jnp.float32),),
        in_specs=[vmem] * 5,
        out_specs=(vmem,) * (2 * cuts + 1),
        scratch_shapes=[pltpu.VMEM(rows.shape, jnp.bfloat16)],
        compiler_params=pltpu.CompilerParams(vmem_limit_bytes=24 * 2**20),
        cost_estimate=pl.CostEstimate(
            flops=2 * Y * count * features * 768,
            bytes_accessed=features * 1536 + Y * count * features * 2,
            transcendentals=0,
        ),
        name="project",
    )(scale, shift, w_mine, w_theirs, rows)
    return outs[:cuts], outs[cuts : 2 * cuts], outs[-1]


def attend_kernel(chunks, place_ref, power_ref, gain_ref, w_head_ref, *refs):
    stacks = (refs[: len(chunks)], refs[len(chunks) : 2 * len(chunks)])
    out_ref, query0, query1, key0, key1, value, root = refs[2 * len(chunks) :]
    c_step = pl.program_id(0)
    my_z, my_c = place_ref[1], place_ref[2]
    all_cols = HD * 2 * Y * Z * C
    head = lax.broadcasted_iota(jnp.int32, (1, 128), 1) < HD

    @pl.when(c_step == 0)
    def _():
        totals = []
        for c in range(C):
            total = None
            for y in range(Y):
                for z in range(Z):
                    term = power_ref[(y * Z + z) * C + c]
                    total = term if total is None else total + term
            totals.append(lax.rsqrt(total / all_cols + 1e-6))
        flip = jnp.broadcast_to(my_c, (16, 128)) == 0
        root[0:16, :] = jnp.where(flip, totals[0], totals[1])
        root[16:32, :] = jnp.where(flip, totals[1], totals[0])
        columns = jnp.transpose(root[...])
        lane = lax.broadcasted_iota(jnp.int32, (128, 32), 1)
        gain_q = gain_ref[0:1, :]
        gain_k = gain_ref[1:2, :]
        for slot_c in range(C):
            for slot_y in range(Y):
                for slot_z in range(Z):
                    z_at = my_z if slot_z == 0 else 1 - my_z
                    at = slot_y * Z + z_at + slot_c * 16
                    scale_q = jnp.sum(jnp.where(lane == at, columns, 0.0), axis=1, keepdims=True)
                    scale_k = jnp.sum(jnp.where(lane == at + 8, columns, 0.0), axis=1, keepdims=True)
                    base = ((slot_c * Y + slot_y) * Z + slot_z) * 128
                    for ref, (kind, a, b) in zip(stacks[slot_c], chunks):
                        if kind != slot_z:
                            continue
                        span = slice(base + a, base + b)
                        unit = (ref[slot_y, :, 0:128] * scale_q[a:b] * gain_q).astype(jnp.bfloat16)
                        query = unit.astype(jnp.float32) * (HD ** (-0.5) * math.log2(math.e))
                        high = query.astype(jnp.bfloat16).astype(jnp.float32)
                        low = pltpu.roll(query - high, HD, 1)
                        query0[span, :] = jnp.where(head, high, low).astype(jnp.bfloat16)
                        query1[span, :] = jnp.where(head, low, high).astype(jnp.bfloat16)
                        keys = ref[slot_y, :, 128:256] * scale_k[a:b] * gain_k
                        turned = pltpu.roll(keys, HD, 1)
                        key0[span, :] = jnp.where(head, keys, turned).astype(jnp.bfloat16)
                        key1[span, :] = jnp.where(head, turned, keys).astype(jnp.bfloat16)
                        value[span, 0:128] = ref[slot_y, :, 256:384].astype(jnp.bfloat16)
        value[:, 128:256] = jnp.ones((value.shape[0], 128), jnp.bfloat16)

    count = Y * Z * 128
    start = pl.multiple_of(c_step * count, count)
    scores = [
        lax.dot_general(
            queries[pl.ds(start, count), :], keys[...], (((1,), (1,)), ((), ())),
            preferred_element_type=jnp.float32,
        )
        for queries, keys in ((query0, key0), (query1, key1))
    ]
    raised = [
        jnp.exp2(part - jnp.max(part, axis=-1, keepdims=True)).astype(jnp.bfloat16)
        for part in scores
    ]
    both = [jnp.dot(part, value[...], preferred_element_type=jnp.float32) for part in raised]
    outs = [part[:, :128] / part[:, 128:] for part in both]
    attended = jnp.where(head, outs[0], outs[1]).astype(jnp.bfloat16)
    partial = lax.dot_general(
        w_head_ref[...], attended, (((0,), (1,)), ((), ())), preferred_element_type=jnp.float32
    ).astype(jnp.bfloat16)
    for y in range(Y):
        at = y * Z * 128
        out_ref[y, 0, my_z] = partial[:, at : at + 128]
        out_ref[y, 0, 1 - my_z] = partial[:, at + 128 : at + 256]


def attend(chunks, place, powers, gains, w_head, mine, theirs):
    tokens = Y * Z * C * 128
    const = lambda rank: (lambda c, place: (0,) * rank)
    stack = [pl.BlockSpec(a.shape, const(3)) for a in (*mine, *theirs)]
    return pl.pallas_call(
        functools.partial(attend_kernel, chunks),
        out_shape=jax.ShapeDtypeStruct((Y, C, Z, 64, 128), jnp.bfloat16),
        grid_spec=pltpu.PrefetchScalarGridSpec(
            num_scalar_prefetch=1,
            grid=(C,),
            in_specs=[
                pl.BlockSpec(powers.shape, const(3)),
                pl.BlockSpec(gains.shape, const(2)),
                pl.BlockSpec((128, LAT), lambda c, place: (place[3], 0)),
                *stack,
            ],
            out_specs=pl.BlockSpec(
                (Y, 1, Z, LAT, 128),
                lambda c, place: (0, lax.rem(c + place[2], C), 0, 0, 0),
            ),
            scratch_shapes=[pltpu.VMEM((tokens, 128), jnp.bfloat16)] * 4
            + [pltpu.VMEM((tokens, 256), jnp.bfloat16), pltpu.VMEM((32, 128), jnp.float32)],
        ),
        compiler_params=pltpu.CompilerParams(vmem_limit_bytes=56 * 2**20),
        cost_estimate=pl.CostEstimate(
            flops=tokens * tokens * 1024, bytes_accessed=2**22, transcendentals=2 * tokens * tokens
        ),
        name="attend",
    )(place, powers, gains, w_head, *mine, *theirs)


def layer_norm(token_rows):
    average = jnp.mean(token_rows, axis=-1, keepdims=True)
    centred = token_rows - average
    spread = jnp.mean(centred * centred, axis=-1, keepdims=True)
    return centred * lax.rsqrt(spread + 1e-06)


def spread_over(value, axis, count, groups=None):
    copies = jnp.broadcast_to(value[None], (count,) + value.shape)
    return lax.all_to_all(copies, axis, 0, 0, axis_index_groups=groups)


def per_device(
    x_start, old_states, hidden, modulation, step_index, sigma_table,
    w_query, w_key, w_value, qk_gain, w_head, w_skip,
):
    seq_rank = lax.axis_index("seq").astype(jnp.int32)
    time_rank = lax.axis_index("tm").astype(jnp.int32)
    my_y, my_z, my_c = seq_rank // (Z * C), (seq_rank // C) % Z, seq_rank % C
    my_x, my_zl = time_rank // ZL, time_rank % ZL
    place = jnp.stack([my_y, my_z, my_c, seq_rank])
    raw = hidden[0]

    far = [lax.ppermute(raw[a:b], "seq", TO_FAR) for a, b in CHUNKS]

    once = lax.optimization_barrier(jnp.int32(1))
    own = lax.fori_loop(
        0, once, lambda _, own: spread_over(raw, "seq", Y, Y_GROUPS), jnp.zeros((Y,) + raw.shape, raw.dtype)
    )
    parts, own = lax.optimization_barrier(((w_query, w_key, w_value), own))
    w_mine = jnp.concatenate(parts, axis=1)
    w_theirs = lax.ppermute(w_mine, "seq", TO_CORE)
    own = own.reshape(-1, raw.shape[1])
    following = jnp.concatenate([step_index[1:], step_index[-1:] + 1])
    step_now = lax.dynamic_index_in_dim(step_index, time_rank, 0, False)
    step_next = lax.dynamic_index_in_dim(following, time_rank, 0, False)
    delta = lax.dynamic_index_in_dim(sigma_table, step_next, 0, False) - (
        lax.dynamic_index_in_dim(sigma_table, step_now, 0, False)
    )
    mod_now = lax.dynamic_index_in_dim(modulation, step_now, 0, False)
    scale, shift = mod_now[0:1], mod_now[1:2]
    own_normed = (layer_norm(raw.astype(jnp.float32)) * (1.0 + scale) + shift).astype(jnp.bfloat16)
    skip = jnp.dot(own_normed, w_skip, preferred_element_type=jnp.float32)

    mine, theirs, powers = [], [], []

    def project_stack(rows, cuts):
        kept, given, power = project(scale, shift, w_mine, w_theirs, rows, cuts)
        mine.extend(kept)
        theirs.extend(lax.ppermute(part, "seq", TO_CORE) for part in given)
        powers.append(power)

    project_stack(own, 1)
    old_here, own_power = lax.optimization_barrier((old_states[0], powers[0]))
    powers[0] = own_power
    old_there = lax.ppermute(old_here, "tm", TO_ACROSS)
    rows, _ = lax.optimization_barrier((far[0], own))
    stack = spread_over(rows, "seq", Y, Y_GROUPS).reshape(-1, raw.shape[1])
    stack, old_there = lax.optimization_barrier((stack, old_there))
    project_stack(stack, 2)
    power_own, power_far = powers
    low = jnp.where(my_z == 0, power_own, power_far)
    high = jnp.where(my_z == 0, power_far, power_own)
    table = jnp.stack([low, high], axis=1).transpose(2, 0, 1, 3).reshape(2 * Y * Z, 128)
    powers = spread_over(table, "seq", Y * Z * C)

    chunks = ((0, 0, 128),) + ((1, 0, 64), (1, 64, 128))
    partial = attend(chunks, place, powers, qk_gain, w_head, mine, theirs)
    partial = partial.reshape(Y * C, Z, LAT, 128)
    partial = lax.all_to_all(partial, "seq", 0, 0, axis_index_groups=YC_GROUPS)
    partial = jnp.sum(partial.astype(jnp.float32), axis=0)
    here = lax.dynamic_index_in_dim(partial, my_z, 0, False) + skip.T
    owner = (jnp.arange(Z) == my_z)[:, None, None]
    sent = jnp.where(owner, here[None], partial).astype(jnp.bfloat16)
    sent = jnp.broadcast_to(sent[:, None], (Z, ZL, LAT, 128)).reshape(Z * ZL, LAT, 128)
    line = lax.all_to_all(sent, ("tm", "seq"), 0, 0, axis_index_groups=Z_GROUPS)
    line = line.reshape(Z, ZL, LAT, 128).astype(jnp.float32)
    there = lax.dynamic_index_in_dim(line, 1 - my_z, 0, False)
    drift = here + lax.dynamic_index_in_dim(there, my_zl, 0, False)
    increment = delta * drift
    steps = jnp.concatenate([step_index, step_index[-1:] + 1])
    sigmas = jnp.dot(
        (steps[:, None] == jnp.arange(sigma_table.shape[0])).astype(jnp.float32), sigma_table,
        precision=lax.Precision.HIGHEST,
    )
    deltas = lax.dynamic_slice_in_dim(sigmas[1:] - sigmas[:-1], my_x * ZL, ZL, 0)
    line = jnp.sum(line, axis=0) * deltas[:, None, None]
    total = jnp.sum(line, axis=0)
    before = (jnp.arange(ZL) < my_zl)[:, None, None]
    earlier = jnp.sum(jnp.where(before, line, 0.0), axis=0)
    x_groups = [[x * ZL + z for x in range(4)] for z in range(ZL)]
    totals = spread_over(total, "tm", 4, x_groups)
    before = (jnp.arange(4) < my_x)[:, None, None]
    entered = jnp.sum(jnp.where(before, totals, 0.0), axis=0) + x_start.T
    new_state = entered + (earlier + increment)
    change = new_state - old_states[0].T
    square = jnp.sum(change * change)
    upto = (jnp.arange(ZL) <= (my_zl + ZL // 2) % ZL)[:, None, None]
    change_there = entered + jnp.sum(jnp.where(upto, line, 0.0), axis=0) - old_there.T
    square_there = jnp.sum(change_there * change_there)
    squares = jnp.where(jnp.arange(Z) == my_z, square, square_there)
    squares = jnp.broadcast_to(squares[:, None, None, None], (Z, Y * C, 1, 128))
    squares = lax.all_to_all(
        squares.reshape(Z * Y * C, 1, 128), ("tm", "seq"), 0, 0, axis_index_groups=ERROR_GROUPS
    )
    error = (jnp.sum(squares[:, 0, 0]) / (Y * Z * C * change.size)).reshape(1)
    return (drift.T[None], new_state.T[None], error)


def solution(mesh):
    return jax.shard_map(
        per_device,
        mesh=mesh,
        in_specs=(
            P("seq", None),
            P("tm", "seq", None),
            P("tm", "seq", None),
            P(),
            P(),
            P(),
            P(None, "seq"),
            P(None, "seq"),
            P(None, "seq"),
            P(None, "seq"),
            P(),
            P(),
        ),
        out_specs=(P("tm", "seq", None), P("tm", "seq", None), P("tm")),
        check_vma=False,
    )
```
